32 devices in a mesh: rep: 8 (over z, x), fsdp: 4 (over y, core).
Axes of the slice: x: 2, y: 2, z: 4, core: 2. Of those that a mesh axis runs over, the one named last changes fastest.
Arguments:
- tokens: bfloat16 [8, 2048, 1024], P('rep', 'fsdp'), may hold values from -6 to 6
- segments: int32 [8, 2048], P('rep'), may hold values from 0 to 5, never falling along the last dimension, each value on 1 to 512 neighbouring positions
- cotangent: bfloat16 [8, 2048, 1024], P('rep', 'fsdp'), may hold values from -6 to 6
- attn_gain: bfloat16 [1024], P('fsdp'), may hold values from 0.5 to 1.5
- query_weight: bfloat16 [1024, 2048], P('fsdp'), may hold values from -0.1875 to 0.1875
- key_weight: bfloat16 [1024, 1024], P('fsdp'), may hold values from -0.1875 to 0.1875
- value_weight: bfloat16 [1024, 1024], P('fsdp'), may hold values from -0.1875 to 0.1875
- query_gain: bfloat16 [128], P('fsdp'), may hold values from 0.5 to 1.5
- key_gain: bfloat16 [128], P('fsdp'), may hold values from 0.5 to 1.5
- out_weight: bfloat16 [2048, 1024], P('fsdp'), may hold values from -0.75 to 0.75
- mlp_gain: bfloat16 [1024], P('fsdp'), may hold values from 0.5 to 1.5
- gate_weight: bfloat16 [1024, 3072], P('fsdp'), may hold values from -0.1875 to 0.1875
- up_weight: bfloat16 [1024, 3072], P('fsdp'), may hold values from -0.1875 to 0.1875
- down_weight: bfloat16 [3072, 1024], P('fsdp'), may hold values from -0.109375 to 0.109375
Outputs:
- output: bfloat16 [8, 2048, 1024], P('rep', 'fsdp')
- tokens_grad: float32 [8, 2048, 1024], P('rep', 'fsdp')
- attn_gain_grad: float32 [1024], P('fsdp')
- query_weight_grad: float32 [1024, 2048], P('fsdp')
- key_weight_grad: float32 [1024, 1024], P('fsdp')
- value_weight_grad: float32 [1024, 1024], P('fsdp')
- query_gain_grad: float32 [128], P('fsdp')
- key_gain_grad: float32 [128], P('fsdp')
- out_weight_grad: float32 [2048, 1024], P('fsdp')
- mlp_gain_grad: float32 [1024], P('fsdp')
- gate_weight_grad: float32 [1024, 3072], P('fsdp')
- up_weight_grad: float32 [1024, 3072], P('fsdp')
- down_weight_grad: float32 [3072, 1024], P('fsdp')
The draws below stay inside these ranges and needn't reach their ends.
Inputs may be any that keep to these rules, and one draw needn't show every extreme that they name: `segments`: segment numbers never fall along a sequence; each of the 6 documents of a sequence has 1 to 512 tokens, and one has exactly 512.
All inputs are finite; a program needn't handle non-finite values.
Results may differ from the reference program's by a relative error of at most 0.02.
Values may be sent and summed in bfloat16 or wider, within the bound.
A program may use at most 192 MiB of HBM per device.

```python
import math
import jax
import jax.numpy as jnp
import numpy as np
from jax import lax

D = 1024
H = 16
KVH = 8
HD = 128
FF = 3072
MOST = 512
SEQ = 2048
DOCS = 6
N_REP = 8


def shard_levels(rng, extent, shards, smallest, top_value):
    def one(axis_at, parts):
        steps = jax.random.uniform(jax.random.fold_in(jax.random.fold_in(rng, 6), axis_at), (parts,), jnp.float32, smallest / len(shards), top_value / len(shards))
        return jnp.repeat(jnp.exp(steps), extent[axis_at] // parts).reshape((-1,) + (1,) * (len(extent) - axis_at - 1))

    gain = one(*shards[0])
    for cut in shards[1:]:
        gain = gain * one(*cut)
    return gain


def length_profile(amount, total, reach, lean):
    weights = [(1 << 20) // math.isqrt(standing ** lean) + 1 for standing in range(2, amount + 1)]
    rest, given = total - reach - (amount - 1), [1] * (amount - 1)
    while rest > 0:
        candidates = [i for i in range(amount - 1) if given[i] < reach]
        pool, budget = sum([weights[i] for i in candidates]), rest
        for i in candidates:
            addition = min(reach - given[i], max(1, budget * weights[i] // pool), rest)
            given[i] = given[i] + addition
            rest = rest - addition
    return np.array([reach] + given)


def ragged_sizes(key, amount, total, reach, lean):
    if amount == 2:
        one = jax.random.randint(key, (), max(1, total - reach), min(reach, total - 1) + 1)
        return jnp.stack([one, total - one])
    tallies = jnp.asarray(length_profile(amount, total, reach, lean), jnp.int32)
    twos = (amount - 1) // 2
    giver, taker = tallies[1:1 + 2 * twos:2], tallies[2:2 + 2 * twos:2]
    margin = jnp.minimum(giver - 1, reach - taker)
    moved = jax.random.randint(jax.random.fold_in(key, 1), (twos,), 0, 1 << 20) % (margin + 1)
    tallies = tallies.at[1:1 + 2 * twos:2].set(giver - moved).at[2:2 + 2 * twos:2].set(taker + moved)
    return tallies[jax.random.permutation(jax.random.fold_in(key, 2), amount)]


def centred(stream_key, extent, scale, bound, shards=(), kind=jnp.bfloat16):
    values = jax.random.normal(stream_key, extent, jnp.float32) * scale
    if len(shards) > 0:
        values = shard_levels(stream_key, extent, shards, -0.22, 0.18) * values
    return jnp.clip(values, min=-bound, max=bound).astype(kind)


def setup_inputs(seed: int = 0) -> dict:
    key_list = jax.random.split(jax.random.key(seed), 15)
    return {
        "tokens": centred(key_list[0], (N_REP, SEQ, D), 1.0, 6.0, ((0, 8), (1, 4))),
        "segments": jax.vmap(lambda own: jnp.searchsorted(jnp.cumsum(ragged_sizes(own, DOCS, SEQ, MOST, 1)), jnp.arange(SEQ), side="right"))(jax.random.split(key_list[1], N_REP)).reshape((N_REP, SEQ)).astype(jnp.int32),
        "cotangent": centred(key_list[2], (N_REP, SEQ, D), 1.0, 6.0, ((0, 8), (1, 4))),
        "attn_gain": jnp.clip(1.0 + 0.1 * jax.random.normal(key_list[3], (D,), jnp.float32), 0.5, 1.5).astype(jnp.bfloat16),
        "query_weight": centred(key_list[4], (D, H * HD), D ** -0.5, 0.1875, ((0, 4),)),
        "key_weight": centred(key_list[5], (D, KVH * HD), D ** -0.5, 0.1875, ((0, 4),)),
        "value_weight": centred(key_list[6], (D, KVH * HD), D ** -0.5, 0.1875, ((0, 4),)),
        "query_gain": jnp.clip(1.0 + 0.1 * jax.random.normal(key_list[7], (HD,), jnp.float32), 0.5, 1.5).astype(jnp.bfloat16),
        "key_gain": jnp.clip(1.0 + 0.1 * jax.random.normal(key_list[8], (HD,), jnp.float32), 0.5, 1.5).astype(jnp.bfloat16),
        "out_weight": centred(key_list[9], (H * HD, D), (H * HD // 32) ** -0.5, 0.75, ((0, 4),)),
        "mlp_gain": jnp.clip(1.0 + 0.1 * jax.random.normal(key_list[10], (D,), jnp.float32), 0.5, 1.5).astype(jnp.bfloat16),
        "gate_weight": centred(key_list[11], (D, FF), D ** -0.5, 0.1875, ((0, 4),)),
        "up_weight": centred(key_list[12], (D, FF), D ** -0.5, 0.1875, ((0, 4),)),
        "down_weight": centred(key_list[13], (FF, D), FF ** -0.5, 0.109375, ((0, 4),)),
    }


EPSILON = 1e-06
ROPE_BASE = 1000000.0
MASKED = -1e+30

@jax.custom_vjp
def low(v):
    return lax.optimization_barrier(v.astype(jnp.bfloat16)).astype(jnp.float32)

@jax.custom_vjp
def low_back(v):
    return v

def low_keep(v):
    return (low(v), None)

def low_pass(kept, grad):
    return (grad,)

def back_keep(v):
    return (v, None)

def back_low(kept, grad):
    return (low(grad),)
low.defvjp(low_keep, low_pass)
low_back.defvjp(back_keep, back_low)

def rms_scale(field, scaling):
    return field * lax.rsqrt(lax.optimization_barrier(jnp.mean(field * field, axis=-1, keepdims=True)) + EPSILON) * scaling

def rotate(field, cosine, sine):
    half_width = field.shape[-1] // 2
    first = field[..., :half_width]
    second = field[..., half_width:]
    return jnp.concatenate([first * cosine - second * sine, second * cosine + first * sine], axis=-1)

def rope_tables(positions, head_width):
    freqs = ROPE_BASE ** (-(jnp.arange(head_width // 2, dtype=jnp.float32) * 2.0 / head_width))
    angle_table = positions[:, None] * freqs[None, :]
    return (jnp.cos(angle_table)[:, None, :], jnp.sin(angle_table)[:, None, :])

def matmul(left, right):
    return jnp.dot(left, right, precision=lax.Precision.HIGHEST)

def attend_block(operands):
    query_block, key_lower, key_upper, value_lower, value_upper, seg_query, seg_lower, seg_upper = operands
    keys = jnp.concatenate([key_lower, key_upper], axis=0)
    values = jnp.concatenate([value_lower, value_upper], axis=0)
    seg_keys = jnp.concatenate([seg_lower, seg_upper], axis=0)
    scores = jnp.einsum('qcgd,kcd->cgqk', query_block, keys, precision=lax.Precision.HIGHEST) * HD ** (-0.5)
    key_offsets = jnp.arange(2 * MOST, dtype=jnp.int32)
    query_offsets = jnp.arange(MOST, dtype=jnp.int32)
    allowed = (seg_keys[None, :] == seg_query[:, None]) & (key_offsets[None, :] - MOST <= query_offsets[:, None])
    scores = low_back(jnp.where(allowed, scores, MASKED))
    probs = low(jax.nn.softmax(scores, axis=-1))
    return jnp.einsum('cgqk,kcd->qcgd', probs, values, precision=lax.Precision.HIGHEST)

def layer(inputs, seg_row, weights):
    attn_g, w_query, w_key, w_value, query_g, key_g, w_out, mlp_g, w_gate, w_upper, w_down = weights
    positions = jnp.arange(SEQ, dtype=jnp.int32).astype(jnp.float32)
    cosine, sine = rope_tables(positions, HD)
    act = low(rms_scale(inputs, attn_g))
    query = low_back(matmul(act, w_query)).reshape(SEQ, H, HD)
    key = low_back(matmul(act, w_key)).reshape(SEQ, KVH, HD)
    value = low(low_back(matmul(act, w_value))).reshape(SEQ, KVH, HD)
    query = low(rotate(rms_scale(query, query_g), cosine, sine))
    key = low(rotate(rms_scale(key, key_g), cosine, sine))
    nblocks = SEQ // MOST
    pad_rows = jnp.zeros((MOST, KVH, HD), jnp.float32)
    key_blocks = jnp.concatenate([pad_rows, key], axis=0).reshape(nblocks + 1, MOST, KVH, HD)
    value_blocks = jnp.concatenate([pad_rows, value], axis=0).reshape(nblocks + 1, MOST, KVH, HD)
    seg_blocks = jnp.concatenate([jnp.full((MOST,), -1, jnp.int32), seg_row]).reshape(nblocks + 1, MOST)
    query_blocks = query.reshape(nblocks, MOST, KVH, H // KVH, HD)
    attended = lax.map(jax.checkpoint(attend_block), (query_blocks, key_blocks[:-1], key_blocks[1:], value_blocks[:-1], value_blocks[1:], seg_row.reshape(nblocks, MOST), seg_blocks[:-1], seg_blocks[1:]))
    mixed = low(low_back(attended.reshape(SEQ, H * HD)))
    hidden = inputs + low_back(matmul(mixed, w_out))
    act2 = low(rms_scale(hidden, mlp_g))
    gate = low_back(matmul(act2, w_gate))
    upper = low_back(matmul(act2, w_upper))
    inner = low(jax.nn.silu(gate) * upper)
    return hidden + low_back(matmul(inner, w_down))

def reference(tokens, segments, cotangent, attn_gain, query_weight, key_weight, value_weight, query_gain, key_gain, out_weight, mlp_gain, gate_weight, up_weight, down_weight):
    params = tuple((item.astype(jnp.float32) for item in (attn_gain, query_weight, key_weight, value_weight, query_gain, key_gain, out_weight, mlp_gain, gate_weight, up_weight, down_weight)))

    def whole(inputs, *weights):

        def one_sequence(operands):
            return layer(operands[0], operands[1], weights)
        return lax.map(one_sequence, (inputs, segments))
    result, pullback = jax.vjp(whole, tokens.astype(jnp.float32), *params)
    grads = pullback(cotangent.astype(jnp.float32))
    return (result.astype(jnp.bfloat16), grads[0], grads[1], grads[2], grads[3], grads[4], grads[5], grads[6], grads[7], grads[8], grads[9], grads[10], grads[11])
```

```python
import functools

import jax
import jax.numpy as jnp
from jax import lax
from jax.experimental import pallas as pl
from jax.experimental.pallas import tpu as pltpu
from jax.sharding import PartitionSpec as P

EPSILON = 1e-06
ROPE_BASE = 1000000.0
MASKED = -1e30
LOG2E = 1.4426950408889634
BF = jnp.bfloat16
F32 = jnp.float32


def mm(a, b, ca=1, cb=0):
    return lax.dot_general(a, b, (((ca,), (cb,)), ((), ())), preferred_element_type=F32)


def flip(value, axis, bit):
    count = lax.axis_size(axis)
    return lax.ppermute(value, axis, [(i, i ^ bit) for i in range(count)])


def own_bit(axis, bit):
    return (lax.axis_index(axis) // bit) % 2


def bits_of(axis):
    count, bits, bit = lax.axis_size(axis), [], 1
    while bit < count:
        bits.append(bit)
        bit *= 2
    return bits


def pair(mine, theirs, upper, axis):
    low = jnp.where(upper, theirs, mine)
    high = jnp.where(upper, mine, theirs)
    return jnp.stack([low, high], axis=axis)


def gather(shard):
    block = shard
    for depth, bit in enumerate(reversed(bits_of("fsdp"))):
        block = pair(block, flip(block, "fsdp", bit), own_bit("fsdp", bit) == 1, depth)
    return block.reshape((-1,) + shard.shape[1:])


def half(blocks, axis, which):
    return lax.dynamic_index_in_dim(blocks, which, axis, keepdims=False)


def scatter_product(rows, cols):
    tokens, width = rows.shape
    count = lax.axis_size("fsdp")
    bits = bits_of("fsdp")
    own = width // count
    mine = own_bit("fsdp", 1)
    split = rows.reshape(tokens, count // 2, 2, own)
    sent = half(split, 2, 1 - mine).reshape(tokens, width // 2)
    kept = half(split, 2, mine).reshape(tokens, width // 2)
    arrived = flip(mm(sent, cols, 0, 0).astype(BF), "fsdp", 1)
    part = (mm(kept, cols, 0, 0) + arrived.astype(F32)).astype(BF)
    for bit in bits[1:]:
        mine = own_bit("fsdp", bit)
        remaining = part.shape[0] // own
        view = part.reshape(remaining // 2, 2, own, -1)
        arrived = flip(half(view, 1, 1 - mine), "fsdp", bit)
        part = (half(view, 1, mine).astype(F32) + arrived.astype(F32)).astype(BF)
        part = part.reshape((remaining // 2) * own, -1)
    return part


def sum_rep(part):
    bits = bits_of("rep")
    shape = part.shape
    for bit in bits:
        mine = own_bit("rep", bit)
        view = part.reshape(2, part.shape[0] // 2, shape[1])
        arrived = flip(half(view, 0, 1 - mine), "rep", bit)
        total = half(view, 0, mine).astype(F32) + arrived.astype(F32)
        part = total.astype(BF)
    for bit in reversed(bits):
        block = pair(part, flip(part, "rep", bit), own_bit("rep", bit) == 1, 0)
        part = block.reshape(-1, shape[1])
    return part.astype(F32)


def sum_all(vector):
    for axis in ("fsdp", "rep"):
        for bit in bits_of(axis):
            vector = vector + flip(vector, axis, bit)
    return vector


def passed_along(value, axis, steps):
    count = lax.axis_size(axis)
    first, last = (max(0, -steps), min(count, count - steps))
    return lax.ppermute(value, axis, [(source, source + steps) for source in range(first, last)])


def rms_scale(field, scaling):
    return field * lax.rsqrt(jnp.mean(field * field, axis=-1, keepdims=True) + EPSILON) * scaling


def rope_tables(positions, head_width):
    freqs = ROPE_BASE ** (-(jnp.arange(head_width // 2, dtype=F32) * 2.0 / head_width))
    angle_table = positions[:, None] * freqs[None, :]
    cosine, sine = jnp.cos(angle_table), jnp.sin(angle_table)
    return (
        jnp.concatenate([cosine, cosine], axis=1),
        jnp.concatenate([-sine, sine], axis=1),
    )


def swap(field):
    return pltpu.roll(field, field.shape[-1] // 2, 1)


def turn(raw, gain, cosine, sine):
    scaled = rms_scale(raw, gain)
    return scaled * cosine + swap(scaled) * sine


def turn_back(raw, gain, cosine, sine, grad):
    inverse = lax.rsqrt(jnp.mean(raw * raw, axis=-1, keepdims=True) + EPSILON)
    unit = raw * inverse
    grad = grad * cosine + swap(grad * sine)
    gain_part = jnp.sum(grad * unit, axis=0, keepdims=True)
    grad = grad * gain
    back = inverse * (grad - unit * jnp.mean(grad * unit, axis=-1, keepdims=True))
    return back, gain_part


def full_spec(shape):
    return pl.BlockSpec(shape, lambda h: (0, 0))


def head_spec(rows, width):
    return pl.BlockSpec((rows, width), lambda h: (0, h))


def params():
    return pltpu.CompilerParams(vmem_limit_bytes=40 * 1024 * 1024)


def turn_kernel(raw, gain, cosine, sine, out):
    out[...] = turn(raw[...], gain[...], cosine[...], sine[...]).astype(BF)


def turn_call(raw, gain, cosine, sine):
    tokens, width = raw.shape
    hd = gain.shape[1]
    return pl.pallas_call(
        turn_kernel,
        grid=(width // hd,),
        in_specs=[
            head_spec(tokens, hd),
            full_spec((1, hd)),
            full_spec((tokens, hd)),
            full_spec((tokens, hd)),
        ],
        out_specs=head_spec(tokens, hd),
        out_shape=jax.ShapeDtypeStruct((tokens, width), BF),
        compiler_params=params(),
        cost_estimate=pl.CostEstimate(
            flops=tokens * width * 10, bytes_accessed=tokens * width * 6, transcendentals=0
        ),
    )(raw, gain, cosine, sine)


def turn_back_kernel(raw, gain, cosine, sine, grad, back, gain_part):
    result, part = turn_back(raw[...], gain[...], cosine[...], sine[...], grad[...])
    back[...] = result.astype(BF)

    @pl.when(pl.program_id(0) == 0)
    def _():
        gain_part[...] = jnp.zeros_like(gain_part)

    gain_part[...] += part


def turn_back_call(raw, gain, cosine, sine, grad):
    tokens, width = raw.shape
    hd = gain.shape[1]
    return pl.pallas_call(
        turn_back_kernel,
        grid=(width // hd,),
        in_specs=[
            head_spec(tokens, hd),
            full_spec((1, hd)),
            full_spec((tokens, hd)),
            full_spec((tokens, hd)),
            head_spec(tokens, hd),
        ],
        out_specs=[head_spec(tokens, hd), full_spec((1, hd))],
        out_shape=[
            jax.ShapeDtypeStruct((tokens, width), BF),
            jax.ShapeDtypeStruct((1, hd), F32),
        ],
        compiler_params=params(),
        cost_estimate=pl.CostEstimate(
            flops=tokens * width * 20, bytes_accessed=tokens * width * 10, transcendentals=0
        ),
    )(raw, gain, cosine, sine, grad)


def tile_bias(seg_query, seg_keys, at, rows, span):
    shape = (rows, span + rows)
    q = lax.broadcasted_iota(jnp.int32, shape, 0)
    k = lax.broadcasted_iota(jnp.int32, shape, 1)
    same = seg_query[pl.ds(at, rows), :] == seg_keys[:, pl.ds(at, span + rows)]
    return jnp.where(same & (k - span <= q), 0.0, MASKED).astype(F32)


def window(tail, own, at, rows):
    return jnp.concatenate([tail[at:, :], own[0 : at + rows, :]], axis=0)


def attend_kernel(rows, q, kt, k, vt, v, segq, segk, out, bias):
    tokens, hd = kt.shape
    scale = hd ** (-0.5) * LOG2E
    tiles = tokens // rows

    @pl.when(pl.program_id(0) == 0)
    def _():
        for i in range(tiles):
            bias[i] = tile_bias(segq, segk, i * rows, rows, tokens)

    for i in range(tiles):
        at = i * rows
        keys = window(kt, k, at, rows)
        values = window(vt, v, at, rows)
        for g in range(q.shape[1] // hd):
            cols = slice(g * hd, (g + 1) * hd)
            s = mm(q[at : at + rows, cols], keys, 1, 1) * scale + bias[i]
            e = jnp.exp2(s)
            inverse = 1.0 / jnp.sum(e, axis=1, keepdims=True)
            p = (e * inverse).astype(BF)
            out[at : at + rows, cols] = mm(p, values).astype(BF)


def attend_call(q, kt, k, vt, v, segq, segk, hd, rows):
    tokens, width = q.shape
    kvh = k.shape[1] // hd
    gw = width // kvh
    return pl.pallas_call(
        functools.partial(attend_kernel, rows),
        grid=(kvh,),
        in_specs=[head_spec(tokens, gw)]
        + [head_spec(tokens, hd)] * 4
        + [full_spec((tokens, 1)), full_spec((1, 2 * tokens))],
        out_specs=head_spec(tokens, gw),
        out_shape=jax.ShapeDtypeStruct((tokens, width), BF),
        scratch_shapes=[pltpu.VMEM((tokens // rows, rows, tokens + rows), F32)],
        compiler_params=params(),
        cost_estimate=pl.CostEstimate(
            flops=4 * tokens * 2 * tokens * width * 3,
            bytes_accessed=tokens * width * 8,
            transcendentals=0,
        ),
    )(q, kt, k, vt, v, segq, segk)


def attend_back_kernel(
    rows, q, kt, k, vt, v, do, raw, gain, cosine, sine, segq, segk,
    back, gain_part, dkt, dk, dvt, dv, bias, dkw, dvw,
):
    tokens, hd = kt.shape
    scale = hd ** (-0.5)
    tiles = tokens // rows
    first = pl.program_id(0) == 0

    @pl.when(first)
    def _():
        gain_part[...] = jnp.zeros_like(gain_part)
        for i in range(tiles):
            bias[i] = tile_bias(segq, segk, i * rows, rows, tokens)

    dkw[...] = jnp.zeros_like(dkw)
    dvw[...] = jnp.zeros_like(dvw)
    for i in range(tiles):
        at = i * rows
        keys = window(kt, k, at, rows)
        values = window(vt, v, at, rows)
        band = slice(at, at + tokens + rows)
        here = slice(at, at + rows)
        for g in range(q.shape[1] // hd):
            cols = slice(g * hd, (g + 1) * hd)
            qt = q[here, cols]
            dot = do[here, cols]
            e = jnp.exp2(mm(qt, keys, 1, 1) * (scale * LOG2E) + bias[i])
            p = e * (1.0 / jnp.sum(e, axis=1, keepdims=True))
            dp = mm(dot, values, 1, 1)
            dvw[band, :] += mm(p.astype(BF), dot, 0, 0)
            centre = jnp.sum(dp * p, axis=1, keepdims=True)
            ds = (p * (dp - centre)).astype(BF)
            dkw[band, :] += mm(ds, qt, 0, 0)
            dq = mm(ds, keys) * scale
            result, part = turn_back(
                raw[here, cols], gain[...], cosine[here, :], sine[here, :], dq
            )
            back[here, cols] = result.astype(BF)
            gain_part[...] += part
    dkt[...] = (dkw[0:tokens, :] * scale).astype(BF)
    dk[...] = dkw[tokens:, :] * scale
    dvt[...] = dvw[0:tokens, :].astype(BF)
    dv[...] = dvw[tokens:, :]


def attend_back_call(q, kt, k, vt, v, do, raw, gain, cosine, sine, segq, segk, hd, rows, start, count):
    tokens, width = q.shape
    kvh = k.shape[1] // hd
    gw = width // kvh

    def shifted(block):
        return pl.BlockSpec((tokens, block), lambda h: (0, h + start))

    kv = jax.ShapeDtypeStruct((tokens, count * hd), F32)
    kv_sent = jax.ShapeDtypeStruct((tokens, count * hd), BF)
    return pl.pallas_call(
        functools.partial(attend_back_kernel, rows),
        grid=(count,),
        in_specs=[shifted(gw)]
        + [shifted(hd)] * 4
        + [
            shifted(gw),
            shifted(gw),
            full_spec((1, hd)),
            full_spec((tokens, hd)),
            full_spec((tokens, hd)),
            full_spec((tokens, 1)),
            full_spec((1, 2 * tokens)),
        ],
        out_specs=[head_spec(tokens, gw), full_spec((1, hd))] + [head_spec(tokens, hd)] * 4,
        out_shape=[
            jax.ShapeDtypeStruct((tokens, count * gw), BF),
            jax.ShapeDtypeStruct((1, hd), F32),
            kv_sent,
            kv,
            kv_sent,
            kv,
        ],
        scratch_shapes=[
            pltpu.VMEM((tokens // rows, rows, tokens + rows), F32),
            pltpu.VMEM((2 * tokens, hd), F32),
            pltpu.VMEM((2 * tokens, hd), F32),
        ],
        compiler_params=params(),
        cost_estimate=pl.CostEstimate(
            flops=10 * tokens * 2 * tokens * count * gw * 2,
            bytes_accessed=tokens * count * gw * 20,
            transcendentals=0,
        ),
    )(q, kt, k, vt, v, do, raw, gain, cosine, sine, segq, segk)


def gating(gate, upper):
    return jax.nn.silu(gate) * upper


def body(
    tokens,
    segments,
    cotangent,
    attn_gain,
    query_weight,
    key_weight,
    value_weight,
    query_gain,
    key_gain,
    out_weight,
    mlp_gain,
    gate_weight,
    up_weight,
    down_weight,
):
    gains = [attn_gain, mlp_gain, query_gain, key_gain]
    packed = gather(jnp.concatenate(gains)[None, :])
    wkey, wvalue, wquery = gather(key_weight), gather(value_weight), gather(query_weight)
    wout, wgate, wupper, wdown = (
        gather(out_weight),
        gather(gate_weight),
        gather(up_weight),
        gather(down_weight),
    )
    whole, at = [], 0
    for item in gains:
        whole.append(packed[:, at : at + item.shape[0]].reshape(-1).astype(F32))
        at += item.shape[0]
    attn_full, mlp_full, qgain, kgain = whole
    qgain, kgain = qgain[None, :], kgain[None, :]
    tok_rows = tokens.shape[1]
    hd = qgain.shape[1]
    kvh = wkey.shape[1] // hd
    rows = min(256, tok_rows)
    place = lax.axis_index("fsdp")
    inputs = tokens[0].astype(F32)
    positions = (place * tok_rows + jnp.arange(tok_rows, dtype=jnp.int32)).astype(F32)
    cosine, sine = rope_tables(positions, hd)
    padded_seg = jnp.concatenate([jnp.full((tok_rows,), -1, jnp.int32), segments[0]])
    window_seg = lax.dynamic_slice_in_dim(padded_seg, place * tok_rows, 2 * tok_rows)
    segk = window_seg[None, :]
    segq = window_seg[tok_rows:, None]
    normed, pull_attn = jax.vjp(rms_scale, inputs, attn_full)
    act = normed.astype(BF)
    key_raw = mm(act, wkey)
    value = mm(act, wvalue).astype(BF)
    key = turn_call(key_raw, kgain, cosine, sine)
    key_tail, value_tail = passed_along(key, "fsdp", 1), passed_along(value, "fsdp", 1)
    query_raw = mm(act, wquery)
    query = turn_call(query_raw, qgain, cosine, sine)
    mixed = attend_call(query, key_tail, key, value_tail, value, segq, segk, hd, rows)
    hidden = inputs + mm(mixed, wout)
    normed2, pull_mlp = jax.vjp(rms_scale, hidden, mlp_full)
    act2 = normed2.astype(BF)
    gate = mm(act2, wgate)
    upper = mm(act2, wupper)
    inner_f, pull_gate = jax.vjp(gating, gate, upper)
    inner = inner_f.astype(BF)
    grad_out = cotangent[0]
    down_part = scatter_product(inner, grad_out)
    final = (hidden + mm(inner, wdown)).astype(BF)
    inner_grad = mm(grad_out, wdown, 1, 1)
    gate_back, upper_back = pull_gate(inner_grad)
    gate_back = gate_back.astype(BF)
    upper_back = upper_back.astype(BF)
    gate_part = scatter_product(act2, gate_back)
    upper_part = scatter_product(act2, upper_back)
    act2_grad = mm(gate_back, wgate, 1, 1) + mm(upper_back, wupper, 1, 1)
    hidden_norm_grad, mlp_gain_part = pull_mlp(act2_grad)
    hidden_grad = grad_out.astype(F32) + hidden_norm_grad
    branch_grad = hidden_grad.astype(BF)
    out_part = scatter_product(mixed, branch_grad)
    mixed_grad = mm(branch_grad, wout, 1, 1).astype(BF)
    groups = 2 if kvh % 2 == 0 else 1
    count = kvh // groups
    gw = query.shape[1] // kvh
    query_gain_part = jnp.zeros((1, hd), F32)
    key_gain_part = jnp.zeros((1, hd), F32)
    act_grad = None
    qkv_parts = []
    for n in range(groups):
        query_back, qpart, dkt, dk, dvt, dv = attend_back_call(
            query, key_tail, key, value_tail, value, mixed_grad, query_raw, qgain,
            cosine, sine, segq, segk, hd, rows, n * count, count,
        )
        own = slice(n * count * hd, (n + 1) * count * hd)
        key_own = dk + passed_along(dkt, "fsdp", -1).astype(F32)
        value_back = (dv + passed_along(dvt, "fsdp", -1).astype(F32)).astype(BF)
        key_back, kpart = turn_back_call(key_raw[:, own], kgain, cosine, sine, key_own)
        query_gain_part = query_gain_part + qpart
        key_gain_part = key_gain_part + kpart
        together = jnp.concatenate([query_back, key_back, value_back], axis=1)
        qkv_parts.append(scatter_product(act, together))
        wide = slice(n * count * gw, (n + 1) * count * gw)
        term = (
            mm(query_back, wquery[:, wide], 1, 1)
            + mm(key_back, wkey[:, own], 1, 1)
            + mm(value_back, wvalue[:, own], 1, 1)
        )
        act_grad = term if act_grad is None else act_grad + term
    input_norm_grad, attn_gain_part = pull_attn(act_grad)
    inputs_grad = hidden_grad + input_norm_grad
    down_sum, gate_sum, upper_sum, out_sum = (
        sum_rep(down_part),
        sum_rep(gate_part),
        sum_rep(upper_part),
        sum_rep(out_part),
    )
    qkv_sums = [sum_rep(part) for part in qkv_parts]
    nq, nk = count * gw, count * hd
    query_sum = jnp.concatenate([s[:, :nq] for s in qkv_sums], axis=1)
    key_sum = jnp.concatenate([s[:, nq : nq + nk] for s in qkv_sums], axis=1)
    value_sum = jnp.concatenate([s[:, nq + nk :] for s in qkv_sums], axis=1)
    vector = jnp.concatenate(
        [attn_gain_part, mlp_gain_part, query_gain_part[0], key_gain_part[0]]
    )
    vector = sum_all(vector)
    parts, at = [], 0
    for item in gains:
        width = item.shape[0]
        parts.append(lax.dynamic_slice_in_dim(vector, at + place * width, width))
        at += width * lax.axis_size("fsdp")
    return (
        final[None],
        inputs_grad[None],
        parts[0],
        query_sum,
        key_sum,
        value_sum,
        parts[2],
        parts[3],
        out_sum,
        parts[1],
        gate_sum,
        upper_sum,
        down_sum,
    )


def solution(mesh):
    in_specs = (
        P("rep", "fsdp", None),
        P("rep", None),
        P("rep", "fsdp", None),
        P("fsdp"),
        P("fsdp", None),
        P("fsdp", None),
        P("fsdp", None),
        P("fsdp"),
        P("fsdp"),
        P("fsdp", None),
        P("fsdp"),
        P("fsdp", None),
        P("fsdp", None),
        P("fsdp", None),
    )
    out_specs = (
        P("rep", "fsdp", None),
        P("rep", "fsdp", None),
        P("fsdp"),
        P("fsdp", None),
        P("fsdp", None),
        P("fsdp", None),
        P("fsdp"),
        P("fsdp"),
        P("fsdp", None),
        P("fsdp"),
        P("fsdp", None),
        P("fsdp", None),
        P("fsdp", None),
    )
    return jax.shard_map(body, mesh=mesh, in_specs=in_specs, out_specs=out_specs, check_vma=False)
```

```python
import functools

import jax
import jax.numpy as jnp
from jax import lax
from jax.experimental import pallas as pl
from jax.experimental.pallas import tpu as pltpu
from jax.sharding import PartitionSpec as P

EPSILON = 1e-06
ROPE_BASE = 1000000.0
MASKED = -1e30
LOG2E = 1.4426950408889634
BF = jnp.bfloat16
F32 = jnp.float32


def mm(a, b, ca=1, cb=0):
    return lax.dot_general(a, b, (((ca,), (cb,)), ((), ())), preferred_element_type=F32)


def flip(value, axis, bit):
    count = lax.axis_size(axis)
    return lax.ppermute(value, axis, [(i, i ^ bit) for i in range(count)])


def own_bit(axis, bit):
    return (lax.axis_index(axis) // bit) % 2


def bits_of(axis):
    count, bits, bit = lax.axis_size(axis), [], 1
    while bit < count:
        bits.append(bit)
        bit *= 2
    return bits


def pair(mine, theirs, upper, axis):
    low = jnp.where(upper, theirs, mine)
    high = jnp.where(upper, mine, theirs)
    return jnp.stack([low, high], axis=axis)


def gather(shard):
    block = shard
    for depth, bit in enumerate(reversed(bits_of("fsdp"))):
        block = pair(block, flip(block, "fsdp", bit), own_bit("fsdp", bit) == 1, depth)
    return block.reshape((-1,) + shard.shape[1:])


def half(blocks, axis, which):
    return lax.dynamic_index_in_dim(blocks, which, axis, keepdims=False)


def scatter_product(rows, cols):
    tokens, width = rows.shape
    count = lax.axis_size("fsdp")
    own = width // count
    mine = own_bit("fsdp", 1)
    split = rows.reshape(tokens, count // 2, 2, own)
    sent = half(split, 2, 1 - mine).reshape(tokens, width // 2)
    kept = half(split, 2, mine).reshape(tokens, width // 2)
    arrived = flip(mm(sent, cols, 0, 0).astype(BF), "fsdp", 1)
    return (mm(kept, cols, 0, 0) + arrived.astype(F32)).astype(BF)


def scatter_rest(part):
    count = lax.axis_size("fsdp")
    own = part.shape[0] * 2 // count
    for bit in bits_of("fsdp")[1:]:
        mine = own_bit("fsdp", bit)
        remaining = part.shape[0] // own
        view = part.reshape(remaining // 2, 2, own, -1)
        arrived = flip(half(view, 1, 1 - mine), "fsdp", bit)
        part = (half(view, 1, mine).astype(F32) + arrived.astype(F32)).astype(BF)
        part = part.reshape((remaining // 2) * own, -1)
    return part


def sum_rep(part):
    bits = bits_of("rep")
    shape = part.shape
    for bit in bits:
        mine = own_bit("rep", bit)
        view = part.reshape(2, part.shape[0] // 2, shape[1])
        arrived = flip(half(view, 0, 1 - mine), "rep", bit)
        total = half(view, 0, mine).astype(F32) + arrived.astype(F32)
        part = total.astype(BF)
    for bit in reversed(bits):
        block = pair(part, flip(part, "rep", bit), own_bit("rep", bit) == 1, 0)
        part = block.reshape(-1, shape[1])
    return part.astype(F32)


def sum_all(vector):
    for axis in ("fsdp", "rep"):
        for bit in bits_of(axis):
            vector = vector + flip(vector, axis, bit)
    return vector


def passed_along(value, axis, steps):
    count = lax.axis_size(axis)
    first, last = (max(0, -steps), min(count, count - steps))
    return lax.ppermute(value, axis, [(source, source + steps) for source in range(first, last)])


def rms_scale(field, scaling):
    return field * lax.rsqrt(jnp.mean(field * field, axis=-1, keepdims=True) + EPSILON) * scaling


def rope_tables(positions, head_width):
    freqs = ROPE_BASE ** (-(jnp.arange(head_width // 2, dtype=F32) * 2.0 / head_width))
    angle_table = positions[:, None] * freqs[None, :]
    cosine, sine = jnp.cos(angle_table), jnp.sin(angle_table)
    return (
        jnp.concatenate([cosine, cosine], axis=1),
        jnp.concatenate([-sine, sine], axis=1),
    )


def swap(field):
    return pltpu.roll(field, field.shape[-1] // 2, 1)


def turn(raw, gain, cosine, sine):
    scaled = rms_scale(raw, gain)
    return scaled * cosine + swap(scaled) * sine


def turn_back(raw, gain, cosine, sine, grad):
    inverse = lax.rsqrt(jnp.mean(raw * raw, axis=-1, keepdims=True) + EPSILON)
    unit = raw * inverse
    grad = grad * cosine + swap(grad * sine)
    gain_part = jnp.sum(grad * unit, axis=0, keepdims=True)
    grad = grad * gain
    back = inverse * (grad - unit * jnp.mean(grad * unit, axis=-1, keepdims=True))
    return back, gain_part


def full_spec(shape):
    return pl.BlockSpec(shape, lambda h: (0, 0))


def head_spec(rows, width):
    return pl.BlockSpec((rows, width), lambda h: (0, h))


def params():
    return pltpu.CompilerParams(vmem_limit_bytes=40 * 1024 * 1024)


def turn_kernel(raw, gain, cosine, sine, out):
    out[...] = turn(raw[...], gain[...], cosine[...], sine[...]).astype(BF)


def turn_call(raw, gain, cosine, sine):
    tokens, width = raw.shape
    hd = gain.shape[1]
    return pl.pallas_call(
        turn_kernel,
        grid=(width // hd,),
        in_specs=[
            head_spec(tokens, hd),
            full_spec((1, hd)),
            full_spec((tokens, hd)),
            full_spec((tokens, hd)),
        ],
        out_specs=head_spec(tokens, hd),
        out_shape=jax.ShapeDtypeStruct((tokens, width), BF),
        compiler_params=params(),
        cost_estimate=pl.CostEstimate(
            flops=tokens * width * 10, bytes_accessed=tokens * width * 6, transcendentals=0
        ),
    )(raw, gain, cosine, sine)


def turn_back_kernel(raw, gain, cosine, sine, grad, back, gain_part):
    result, part = turn_back(raw[...], gain[...], cosine[...], sine[...], grad[...])
    back[...] = result.astype(BF)

    @pl.when(pl.program_id(0) == 0)
    def _():
        gain_part[...] = jnp.zeros_like(gain_part)

    gain_part[...] += part


def turn_back_call(raw, gain, cosine, sine, grad):
    tokens, width = raw.shape
    hd = gain.shape[1]
    return pl.pallas_call(
        turn_back_kernel,
        grid=(width // hd,),
        in_specs=[
            head_spec(tokens, hd),
            full_spec((1, hd)),
            full_spec((tokens, hd)),
            full_spec((tokens, hd)),
            head_spec(tokens, hd),
        ],
        out_specs=[head_spec(tokens, hd), full_spec((1, hd))],
        out_shape=[
            jax.ShapeDtypeStruct((tokens, width), BF),
            jax.ShapeDtypeStruct((1, hd), F32),
        ],
        compiler_params=params(),
        cost_estimate=pl.CostEstimate(
            flops=tokens * width * 20, bytes_accessed=tokens * width * 10, transcendentals=0
        ),
    )(raw, gain, cosine, sine, grad)


def tile_bias(seg_query, seg_keys, at, rows, span):
    shape = (rows, span + rows)
    q = lax.broadcasted_iota(jnp.int32, shape, 0)
    k = lax.broadcasted_iota(jnp.int32, shape, 1)
    same = seg_query[pl.ds(at, rows), :] == seg_keys[:, pl.ds(at, span + rows)]
    return jnp.where(same & (k - span <= q), 0.0, MASKED).astype(F32)


def window(tail, own, at, rows):
    return jnp.concatenate([tail[at:, :], own[0 : at + rows, :]], axis=0)


def attend_kernel(rows, q, kt, k, vt, v, segq, segk, out, bias):
    tokens, hd = kt.shape
    scale = hd ** (-0.5) * LOG2E
    tiles = tokens // rows

    @pl.when(pl.program_id(0) == 0)
    def _():
        for i in range(tiles):
            bias[i] = tile_bias(segq, segk, i * rows, rows, tokens)

    for i in range(tiles):
        at = i * rows
        keys = window(kt, k, at, rows)
        values = window(vt, v, at, rows)
        for g in range(q.shape[1] // hd):
            cols = slice(g * hd, (g + 1) * hd)
            s = mm(q[at : at + rows, cols], keys, 1, 1) * scale + bias[i]
            e = jnp.exp2(s)
            inverse = 1.0 / jnp.sum(e, axis=1, keepdims=True)
            p = (e * inverse).astype(BF)
            out[at : at + rows, cols] = mm(p, values).astype(BF)


def attend_call(q, kt, k, vt, v, segq, segk, hd, rows):
    tokens, width = q.shape
    kvh = k.shape[1] // hd
    gw = width // kvh
    return pl.pallas_call(
        functools.partial(attend_kernel, rows),
        grid=(kvh,),
        in_specs=[head_spec(tokens, gw)]
        + [head_spec(tokens, hd)] * 4
        + [full_spec((tokens, 1)), full_spec((1, 2 * tokens))],
        out_specs=head_spec(tokens, gw),
        out_shape=jax.ShapeDtypeStruct((tokens, width), BF),
        scratch_shapes=[pltpu.VMEM((tokens // rows, rows, tokens + rows), F32)],
        compiler_params=params(),
        cost_estimate=pl.CostEstimate(
            flops=4 * tokens * 2 * tokens * width * 3,
            bytes_accessed=tokens * width * 8,
            transcendentals=0,
        ),
    )(q, kt, k, vt, v, segq, segk)


def attend_back_kernel(
    rows, q, kt, k, vt, v, do, raw, gain, cosine, sine, segq, segk,
    back, gain_part, dkt, dk, dvt, dv, bias, dkw, dvw,
):
    tokens, hd = kt.shape
    scale = hd ** (-0.5)
    tiles = tokens // rows
    first = pl.program_id(0) == 0

    @pl.when(first)
    def _():
        gain_part[...] = jnp.zeros_like(gain_part)
        for i in range(tiles):
            bias[i] = tile_bias(segq, segk, i * rows, rows, tokens)

    dkw[...] = jnp.zeros_like(dkw)
    dvw[...] = jnp.zeros_like(dvw)
    for i in range(tiles):
        at = i * rows
        keys = window(kt, k, at, rows)
        values = window(vt, v, at, rows)
        band = slice(at, at + tokens + rows)
        here = slice(at, at + rows)
        for g in range(q.shape[1] // hd):
            cols = slice(g * hd, (g + 1) * hd)
            qt = q[here, cols]
            dot = do[here, cols]
            e = jnp.exp2(mm(qt, keys, 1, 1) * (scale * LOG2E) + bias[i])
            p = e * (1.0 / jnp.sum(e, axis=1, keepdims=True))
            dp = mm(dot, values, 1, 1)
            dvw[band, :] += mm(p.astype(BF), dot, 0, 0)
            centre = jnp.sum(dp * p, axis=1, keepdims=True)
            ds = (p * (dp - centre)).astype(BF)
            dkw[band, :] += mm(ds, qt, 0, 0)
            dq = mm(ds, keys) * scale
            result, part = turn_back(
                raw[here, cols], gain[...], cosine[here, :], sine[here, :], dq
            )
            back[here, cols] = result.astype(BF)
            gain_part[...] += part
    dkt[...] = (dkw[0:tokens, :] * scale).astype(BF)
    dk[...] = dkw[tokens:, :] * scale
    dvt[...] = dvw[0:tokens, :].astype(BF)
    dv[...] = dvw[tokens:, :]


def attend_back_call(q, kt, k, vt, v, do, raw, gain, cosine, sine, segq, segk, hd, rows, start, count):
    tokens, width = q.shape
    kvh = k.shape[1] // hd
    gw = width // kvh

    def shifted(block):
        return pl.BlockSpec((tokens, block), lambda h: (0, h + start))

    kv = jax.ShapeDtypeStruct((tokens, count * hd), F32)
    kv_sent = jax.ShapeDtypeStruct((tokens, count * hd), BF)
    return pl.pallas_call(
        functools.partial(attend_back_kernel, rows),
        grid=(count,),
        in_specs=[shifted(gw)]
        + [shifted(hd)] * 4
        + [
            shifted(gw),
            shifted(gw),
            full_spec((1, hd)),
            full_spec((tokens, hd)),
            full_spec((tokens, hd)),
            full_spec((tokens, 1)),
            full_spec((1, 2 * tokens)),
        ],
        out_specs=[head_spec(tokens, gw), full_spec((1, hd))] + [head_spec(tokens, hd)] * 4,
        out_shape=[
            jax.ShapeDtypeStruct((tokens, count * gw), BF),
            jax.ShapeDtypeStruct((1, hd), F32),
            kv_sent,
            kv,
            kv_sent,
            kv,
        ],
        scratch_shapes=[
            pltpu.VMEM((tokens // rows, rows, tokens + rows), F32),
            pltpu.VMEM((2 * tokens, hd), F32),
            pltpu.VMEM((2 * tokens, hd), F32),
        ],
        compiler_params=params(),
        cost_estimate=pl.CostEstimate(
            flops=10 * tokens * 2 * tokens * count * gw * 2,
            bytes_accessed=tokens * count * gw * 20,
            transcendentals=0,
        ),
    )(q, kt, k, vt, v, do, raw, gain, cosine, sine, segq, segk)


def gating(gate, upper):
    return jax.nn.silu(gate) * upper


def body(
    tokens,
    segments,
    cotangent,
    attn_gain,
    query_weight,
    key_weight,
    value_weight,
    query_gain,
    key_gain,
    out_weight,
    mlp_gain,
    gate_weight,
    up_weight,
    down_weight,
):
    gains = [attn_gain, mlp_gain, query_gain, key_gain]
    packed = gather(jnp.concatenate(gains)[None, :])
    wkey, wvalue, wquery = gather(key_weight), gather(value_weight), gather(query_weight)
    wout, wgate, wupper, wdown = (
        gather(out_weight),
        gather(gate_weight),
        gather(up_weight),
        gather(down_weight),
    )
    whole, at = [], 0
    for item in gains:
        whole.append(packed[:, at : at + item.shape[0]].reshape(-1).astype(F32))
        at += item.shape[0]
    attn_full, mlp_full, qgain, kgain = whole
    qgain, kgain = qgain[None, :], kgain[None, :]
    tok_rows = tokens.shape[1]
    hd = qgain.shape[1]
    kvh = wkey.shape[1] // hd
    rows = min(256, tok_rows)
    place = lax.axis_index("fsdp")
    inputs = tokens[0].astype(F32)
    positions = (place * tok_rows + jnp.arange(tok_rows, dtype=jnp.int32)).astype(F32)
    cosine, sine = rope_tables(positions, hd)
    padded_seg = jnp.concatenate([jnp.full((tok_rows,), -1, jnp.int32), segments[0]])
    window_seg = lax.dynamic_slice_in_dim(padded_seg, place * tok_rows, 2 * tok_rows)
    segk = window_seg[None, :]
    segq = window_seg[tok_rows:, None]
    normed, pull_attn = jax.vjp(rms_scale, inputs, attn_full)
    act = normed.astype(BF)
    key_raw = mm(act, wkey)
    value = mm(act, wvalue).astype(BF)
    key = turn_call(key_raw, kgain, cosine, sine)
    key_tail, value_tail = passed_along(key, "fsdp", 1), passed_along(value, "fsdp", 1)
    query_raw = mm(act, wquery)
    query = turn_call(query_raw, qgain, cosine, sine)
    mixed = attend_call(query, key_tail, key, value_tail, value, segq, segk, hd, rows)
    hidden = inputs + mm(mixed, wout)
    normed2, pull_mlp = jax.vjp(rms_scale, hidden, mlp_full)
    act2 = normed2.astype(BF)
    gate = mm(act2, wgate)
    upper = mm(act2, wupper)
    inner_f, pull_gate = jax.vjp(gating, gate, upper)
    inner = inner_f.astype(BF)
    grad_out = cotangent[0]
    down_part = scatter_product(inner, grad_out)
    grad_out, down_part = lax.optimization_barrier((grad_out, down_part))
    down_part = scatter_rest(down_part)
    final = (hidden + mm(inner, wdown)).astype(BF)
    inner_grad = mm(grad_out, wdown, 1, 1)
    gate_back, upper_back = pull_gate(inner_grad)
    gate_back = gate_back.astype(BF)
    upper_back = upper_back.astype(BF)
    gate_part = scatter_product(act2, gate_back)
    upper_part = scatter_product(act2, upper_back)
    gate_back, upper_back, gate_part, upper_part = lax.optimization_barrier(
        (gate_back, upper_back, gate_part, upper_part)
    )
    gate_part, upper_part = scatter_rest(gate_part), scatter_rest(upper_part)
    act2_grad = mm(gate_back, wgate, 1, 1) + mm(upper_back, wupper, 1, 1)
    hidden_norm_grad, mlp_gain_part = pull_mlp(act2_grad)
    hidden_grad = grad_out.astype(F32) + hidden_norm_grad
    branch_grad = hidden_grad.astype(BF)
    out_part = scatter_product(mixed, branch_grad)
    mixed_grad = mm(branch_grad, wout, 1, 1).astype(BF)
    mixed_grad, out_part, down_part = lax.optimization_barrier((mixed_grad, out_part, down_part))
    out_part = scatter_rest(out_part)
    groups = 2 if kvh % 2 == 0 else 1
    count = kvh // groups
    gw = query.shape[1] // kvh
    query_gain_part = jnp.zeros((1, hd), F32)
    key_gain_part = jnp.zeros((1, hd), F32)
    act_grad = None
    qkv_parts = []
    for n in range(groups):
        query_back, qpart, dkt, dk, dvt, dv = attend_back_call(
            query, key_tail, key, value_tail, value, mixed_grad, query_raw, qgain,
            cosine, sine, segq, segk, hd, rows, n * count, count,
        )
        if n == 0:
            mixed_grad, gate_part, dkt = lax.optimization_barrier((mixed_grad, gate_part, dkt))
        own = slice(n * count * hd, (n + 1) * count * hd)
        key_own = dk + passed_along(dkt, "fsdp", -1).astype(F32)
        value_back = (dv + passed_along(dvt, "fsdp", -1).astype(F32)).astype(BF)
        key_back, kpart = turn_back_call(key_raw[:, own], kgain, cosine, sine, key_own)
        query_gain_part = query_gain_part + qpart
        key_gain_part = key_gain_part + kpart
        together = jnp.concatenate([query_back, key_back, value_back], axis=1)
        qkv_parts.append(scatter_rest(scatter_product(act, together)))
        wide = slice(n * count * gw, (n + 1) * count * gw)
        term = (
            mm(query_back, wquery[:, wide], 1, 1)
            + mm(key_back, wkey[:, own], 1, 1)
            + mm(value_back, wvalue[:, own], 1, 1)
        )
        act_grad = term if act_grad is None else act_grad + term
    input_norm_grad, attn_gain_part = pull_attn(act_grad)
    inputs_grad = hidden_grad + input_norm_grad
    down_sum, gate_sum, upper_sum, out_sum = (
        sum_rep(down_part),
        sum_rep(gate_part),
        sum_rep(upper_part),
        sum_rep(out_part),
    )
    qkv_sums = [sum_rep(part) for part in qkv_parts]
    nq, nk = count * gw, count * hd
    query_sum = jnp.concatenate([s[:, :nq] for s in qkv_sums], axis=1)
    key_sum = jnp.concatenate([s[:, nq : nq + nk] for s in qkv_sums], axis=1)
    value_sum = jnp.concatenate([s[:, nq + nk :] for s in qkv_sums], axis=1)
    vector = jnp.concatenate(
        [attn_gain_part, mlp_gain_part, query_gain_part[0], key_gain_part[0]]
    )
    vector = sum_all(vector)
    parts, at = [], 0
    for item in gains:
        width = item.shape[0]
        parts.append(lax.dynamic_slice_in_dim(vector, at + place * width, width))
        at += width * lax.axis_size("fsdp")
    return (
        final[None],
        inputs_grad[None],
        parts[0],
        query_sum,
        key_sum,
        value_sum,
        parts[2],
        parts[3],
        out_sum,
        parts[1],
        gate_sum,
        upper_sum,
        down_sum,
    )


def solution(mesh):
    in_specs = (
        P("rep", "fsdp", None),
        P("rep", None),
        P("rep", "fsdp", None),
        P("fsdp"),
        P("fsdp", None),
        P("fsdp", None),
        P("fsdp", None),
        P("fsdp"),
        P("fsdp"),
        P("fsdp", None),
        P("fsdp"),
        P("fsdp", None),
        P("fsdp", None),
        P("fsdp", None),
    )
    out_specs = (
        P("rep", "fsdp", None),
        P("rep", "fsdp", None),
        P("fsdp"),
        P("fsdp", None),
        P("fsdp", None),
        P("fsdp", None),
        P("fsdp"),
        P("fsdp"),
        P("fsdp", None),
        P("fsdp"),
        P("fsdp", None),
        P("fsdp", None),
        P("fsdp", None),
    )
    return jax.shard_map(body, mesh=mesh, in_specs=in_specs, out_specs=out_specs, check_vma=False)
```
